128 devices in a mesh: particle: 16 (over x, y_hi, core), classes: 4 (over z), orient: 2 (over y_lo).
Axes of the slice: x: 4, y: 4 (y_hi: 2, y_lo: 2; y = y_hi * 2 + y_lo), z: 4, core: 2. Of those that a mesh axis runs over, the one named last changes fastest.
Arguments:
- images: bfloat16 [12288, 16384], P('particle'), may hold values from -28 to 28, as said below
- ctf_table: float32 [8, 16384], replicated, may hold values from -1 to 1
- defocus: int32 [12288], P('particle'), may hold values from 0 to 7
- shifts: int32 [12288, 2], P('particle'), may hold values from -8 to 8
- noise_var: float32 [16384], replicated, may hold values from 0.5 to 4
- tau: float32 [16384], replicated, may hold values from 0.5 to 2
- bank: bfloat16 [8, 128, 16384], P('classes', ('particle', 'orient')), may hold values from -0.125 to 0.125
Outputs:
- recon: float32 [8, 128, 16384], P('classes', ('particle', 'orient'))
- loglik: float32 [12288], P('particle')
The draws below stay inside these ranges and needn't reach their ends.
Inputs may be any that keep to these rules, and one draw needn't show every extreme that they name: `images`: rows may differ in scale.
All inputs are finite; a program needn't handle non-finite values.
Results may differ from the reference program's by a relative error of at most 0.02.
Values may be sent and summed in bfloat16 or wider, within the bound.
A program may use at most 256 MiB of HBM per device.

```python
import math
import jax
import jax.numpy as jnp
from jax import lax

BOX = 128
P_SIZE = 16384
I_DEV = 768
NBINS = 8
SHIFT = 8
PARTICLES = 12288
K = 8
J = 128
N_PARTICLE = 16


def draw_images(key, part):
    key = jax.random.fold_in(key, 1)
    values = jnp.clip(jax.random.normal(key, (PARTICLES, P_SIZE), jnp.float32), -6.0, 6.0)
    return values.astype(jnp.bfloat16)


def set_ends(drawn, rng, low, top_value):
    longest = drawn.shape.index(max(drawn.shape))
    spots = []
    for shift in (0, 1):
        where = [jax.random.randint(jax.random.fold_in(rng, axis), (), 0, length) for axis, length in enumerate(drawn.shape)]
        where[longest] = (where[longest] + shift) % drawn.shape[longest]
        spots.append(tuple(where))
    return drawn.at[spots[0]].set(low).at[spots[1]].set(top_value)


def block_scale(own_key, shape, shards, low, top_value):
    gain = 1.0
    for position, blocks in shards:
        heights = jax.random.uniform(jax.random.fold_in(jax.random.fold_in(own_key, 6), position), (blocks,), jnp.float32, low / len(shards), top_value / len(shards))
        gain = gain * jnp.repeat(jnp.exp(heights), shape[position] // blocks).reshape((-1,) + (1,) * (len(shape) - 1 - position))
    return gain


def noise(stream_key, shape, scale, bound, cuts=(), kind=jnp.bfloat16):
    drawn = scale * jax.random.normal(stream_key, shape, jnp.float32)
    if cuts:
        drawn = drawn * block_scale(stream_key, shape, cuts, -0.22, 0.18)
    return jnp.clip(drawn, -bound, bound).astype(kind)


def setup_inputs(seed: int = 0) -> dict:
    key_of = jax.random.split(jax.random.key(seed), 8)
    images = draw_images(jax.random.fold_in(key_of[7], 71), 0)
    ctf_table = jnp.clip(jax.random.uniform(key_of[1], (NBINS, P_SIZE), jnp.float32, -1.0, 1.0), -1.0, 1.0)
    defocus = set_ends(jax.random.randint(key_of[2], (PARTICLES,), 0, NBINS), jax.random.fold_in(key_of[2], 1), 0, NBINS - 1).astype(jnp.int32)
    shifts = set_ends(jax.random.randint(key_of[3], (PARTICLES, 2), -SHIFT, SHIFT + 1), jax.random.fold_in(key_of[3], 1), -SHIFT, SHIFT).astype(jnp.int32)
    noise_var = jnp.clip(jnp.exp(jax.random.uniform(key_of[4], (P_SIZE,), jnp.float32, math.log(0.5), math.log(4.0))), 0.5, 4.0)
    tau = jnp.clip(jnp.exp(jax.random.uniform(key_of[5], (P_SIZE,), jnp.float32, math.log(0.5), math.log(2.0))), 0.5, 2.0)
    bank = noise(key_of[6], (K, J, P_SIZE), (P_SIZE // 8) ** -0.5, 0.125, ((0, 4), (1, 32)))
    return dict(images=images, ctf_table=ctf_table, defocus=defocus, shifts=shifts, noise_var=noise_var, tau=tau, bank=bank)


def shift_images(images, shifts):
    half = BOX // 2
    count = BOX * half
    index = jnp.arange(count, dtype=jnp.int32)
    freq_x = (index % half).astype(jnp.float32)
    row = index // half
    freq_y = jnp.where(row < half, row, row - BOX).astype(jnp.float32)
    angle = (2.0 * math.pi / BOX) * (shifts[:, 0:1].astype(jnp.float32) * freq_x[None, :] + shifts[:, 1:2].astype(jnp.float32) * freq_y[None, :])
    cosine = jnp.cos(angle)
    sine = jnp.sin(angle)
    real_part = images[:, :count].astype(jnp.float32)
    imag_part = images[:, count:].astype(jnp.float32)
    return jnp.concatenate([real_part * cosine - imag_part * sine, real_part * sine + imag_part * cosine], axis=1)


def reference(images, ctf_table, defocus, shifts, noise_var, tau, bank):
    shifted = shift_images(images, shifts)
    ctf = ctf_table[defocus]
    inverse = 1.0 / noise_var
    xs_rows = (shifted * ctf * inverse[None, :]).astype(jnp.bfloat16)
    cs_rows = (0.5 * ctf * ctf * inverse[None, :]).astype(jnp.bfloat16)
    xc_rows = (shifted * ctf).astype(jnp.bfloat16)
    offset = jnp.sum(0.5 * shifted * shifted * inverse[None, :], axis=1)
    bank_f = bank.astype(jnp.float32)
    squared = (bank_f * bank_f).astype(jnp.bfloat16)
    scores = jnp.einsum("ip,kjp->ikj", xs_rows.astype(jnp.float32), bank_f) - jnp.einsum("ip,kjp->ikj", cs_rows.astype(jnp.float32), squared.astype(jnp.float32))
    top = jnp.max(scores, axis=(1, 2))
    expo = jnp.exp(scores - top[:, None, None])
    total = jnp.sum(expo, axis=(1, 2))
    loglik = top + jnp.log(total) - offset
    weights = (expo / total[:, None, None]).astype(jnp.bfloat16)
    slab_w = weights.astype(jnp.float32).reshape(N_PARTICLE, I_DEV, K, J)
    slab_x = xc_rows.astype(jnp.float32).reshape(N_PARTICLE, I_DEV, P_SIZE)

    def add_slab(carry, pair):
        term = jnp.einsum("ikj,ip->kjp", pair[0], pair[1])
        term = lax.optimization_barrier(term.astype(jnp.bfloat16))
        return carry + term.astype(jnp.float32), None

    data, _ = lax.scan(add_slab, jnp.zeros((K, J, P_SIZE), jnp.float32), (slab_w, slab_x))
    onehot = (defocus[:, None] == jnp.arange(NBINS, dtype=jnp.int32)[None, :]).astype(jnp.float32)
    bins = jnp.einsum("ib,ikj->bkj", onehot, weights.astype(jnp.float32), precision=lax.Precision.HIGHEST)
    wgt = jnp.einsum("bkj,bp->kjp", bins, ctf_table * ctf_table, precision=lax.Precision.HIGHEST)
    recon = data / (wgt + tau[None, None, :])
    return recon, loglik
```

```python
import math

import jax
import jax.numpy as jnp
from jax import lax
from jax.experimental import pallas as pl
from jax.experimental.pallas import tpu as pltpu
from jax.sharding import PartitionSpec as P

MESH = pl.DeviceIdType.MESH
BOX = 128
F32 = jnp.float32
BF16 = jnp.bfloat16
NT = (((1,), (1,)), ((), ()))
CHUNKS = 8


def pick_rows(table, index):
    parts = [
        jnp.take_along_axis(table, index[s : s + 8], axis=0, mode="promise_in_bounds")
        for s in range(0, index.shape[0], 8)
    ]
    return parts[0] if len(parts) == 1 else jnp.concatenate(parts, axis=0)


def kernel(
    images, ctf, noise, tau, bank, cos0, sin0, rcos, rsin, bin_lanes, bin_row,
    recon, loglik,
    xc, gathered, cst, sst, off, acc, csq, scaled, squared, scores, wt, msg, msgs, binsend, binrecv, binsum,
    part, sib, ring, fin,
    img_sem, loc_sem, ysend, yrecv, rsend, rrecv, ssend, srecv,
    msend, mrecv, bsend, brecv, psend, precv, qsend, qrecv, fsend, frecv,
):
    rows, size = xc.shape
    half = size // 2
    width = half // CHUNKS
    tiles = width // 128

    me = lax.axis_index("particle")
    cls = lax.axis_index("classes")
    ori = lax.axis_index("orient")
    core = me % 2
    yh = (me // 2) % 2
    x = me // 4
    turn = 3 + 2 * core
    nxt = (((x + 1 + 2 * core) % 4) * 2 + yh) * 2 + core
    prv = (((x + 3 + 2 * core) % 4) * 2 + yh) * 2 + core
    sibling = me + 1 - 2 * core
    partner = me + 2 - 4 * yh
    own = core * 8 + x * 2 + yh
    share = cls * 2 + ori

    def cols(c, base=0):
        return pl.ds(pl.multiple_of(base + c * width, width), width)

    def img_copy(h, c):
        where = cols(c, h * half)
        return pltpu.make_async_copy(images.at[:, where], xc.at[:, where], img_sem.at[h, c])

    def start_images(c, _):
        img_copy(0, c).start()
        img_copy(1, c).start()
        return 0

    lax.fori_loop(0, CHUNKS, start_images, 0)

    def share_device(s):
        return {"classes": s // 2, "orient": s % 2}

    barrier = pltpu.get_barrier_semaphore()
    for k in range(1, 16):
        pl.semaphore_signal(barrier, inc=1, device_id={"particle": (me + k) % 16}, device_id_type=MESH)
    for k in range(1, 8):
        pl.semaphore_signal(barrier, inc=1, device_id=share_device((share + k) % 8), device_id_type=MESH)
    pl.semaphore_wait(barrier, 22)

    def remote(src, dst, send, recv, to):
        return pltpu.make_async_remote_copy(
            src_ref=src, dst_ref=dst, send_sem=send, recv_sem=recv, device_id=to, device_id_type=MESH
        )

    def y_copy(c):
        return remote(
            bank.at[:, cols(c)], gathered.at[own, :, cols(c)], ysend.at[c], yrecv.at[c], {"particle": partner}
        )

    def pair(t, c):
        return gathered.at[pl.ds(core * 8 + ((x + t * turn) % 4) * 2, 2), :, cols(c)]

    def ring_copy(t, c):
        return remote(pair(t, c), pair(t, c), rsend.at[t, c], rrecv.at[t, c], {"particle": nxt})

    def sib_copy(t, c):
        return remote(pair(t, c), pair(t, c), ssend.at[t, c], srecv.at[t, c], {"particle": sibling})

    def start_y(c, _):
        y_copy(c).start()
        return 0

    lax.fori_loop(0, CHUNKS, start_y, 0)
    mine = pltpu.make_async_copy(bank, gathered.at[own], loc_sem)
    mine.start()
    cst[...] = cos0[...]
    sst[...] = sin0[...]
    off[...] = jnp.zeros_like(off)
    acc[...] = jnp.zeros_like(acc)
    csq[...] = jnp.zeros_like(csq)
    mine.wait()

    def shift_chunk(c, with_offset):
        def group(g, _):
            where = pl.ds(pl.multiple_of(g * 16, 16), 16)
            cosine, sine = cst[where, :], sst[where, :]
            step_c, step_s = rcos[where, :], rsin[where, :]
            index = bin_lanes[where, :]
            total = off[where, :] if with_offset else None
            for j in range(tiles):
                at_re = pl.ds(pl.multiple_of(c * width + j * 128, 128), 128)
                at_im = pl.ds(pl.multiple_of(half + c * width + j * 128, 128), 128)
                re = xc[where, at_re].astype(F32)
                im = xc[where, at_im].astype(F32)
                out_re = re * cosine - im * sine
                out_im = re * sine + im * cosine
                if with_offset:
                    total = total + out_re * out_re * (0.5 / noise[:, at_re])
                    total = total + out_im * out_im * (0.5 / noise[:, at_im])
                xc[where, at_re] = (out_re * pick_rows(ctf[:, at_re], index)).astype(BF16)
                xc[where, at_im] = (out_im * pick_rows(ctf[:, at_im], index)).astype(BF16)
                cosine, sine = cosine * step_c - sine * step_s, sine * step_c + cosine * step_s
            cst[where, :] = cosine
            sst[where, :] = sine
            if with_offset:
                off[where, :] = total
            return 0

        lax.fori_loop(0, rows // 16, group, 0)

    def first(n, _):
        @pl.when(n < CHUNKS)
        def _():
            y_copy(n).wait_recv()
            ring_copy(0, n).start()
            sib_copy(0, n).start()

        for t in range(1, 4):
            c = n - t

            @pl.when((c >= 0) & (c < CHUNKS))
            def _():
                ring_copy(t - 1, c).wait_recv()
                if t < 3:
                    ring_copy(t, c).start()
                sib_copy(t, c).start()

        @pl.when(n < CHUNKS)
        def _():
            img_copy(0, n).wait()
            img_copy(1, n).wait()

            @pl.when(n == share)
            def _():
                shift_chunk(n, True)

            @pl.when(n != share)
            def _():
                shift_chunk(n, False)

        return 0

    lax.fori_loop(0, CHUNKS + 3, first, 0)

    def score(c, _):
        for t in range(4):
            sib_copy(t, c).wait_recv()
        for h in range(2):
            at = cols(c, h * half)
            inverse = 1.0 / noise[:, at]

            def prepare(m, _):
                b0 = gathered[2 * m, :, cols(c)].astype(F32)
                b1 = gathered[2 * m + 1, :, cols(c)].astype(F32)
                b = jnp.concatenate([b0[h * 8 : h * 8 + 8], b1[h * 8 : h * 8 + 8]], axis=0)
                value = b * inverse
                high = value.astype(BF16)
                to = pl.multiple_of(m * 16, 16)
                scaled[pl.ds(to, 16), h * width : (h + 1) * width] = high
                scaled[pl.ds(128 + to, 16), h * width : (h + 1) * width] = (value - high.astype(F32)).astype(BF16)
                squared[pl.ds(to, 16), h * width : (h + 1) * width] = (b * b).astype(BF16)
                return 0

            lax.fori_loop(0, 8, prepare, 0)
            table = ctf[:, at]
            cs = 0.5 * table * table * inverse
            cs = jnp.concatenate([cs, cs], axis=0).astype(BF16)
            csq[...] += lax.dot_general(
                cs, squared[:, h * width : (h + 1) * width], NT, preferred_element_type=F32
            )

        def block(r, _):
            where = pl.ds(pl.multiple_of(r * 256, 256), 256)
            acc[where, :] += lax.dot_general(
                xc[where, cols(c)], scaled[:, :width], NT, preferred_element_type=F32
            ) + lax.dot_general(xc[where, cols(c, half)], scaled[:, width:], NT, preferred_element_type=F32)
            return 0

        lax.fori_loop(0, rows // 256, block, 0)
        return 0

    lax.fori_loop(0, CHUNKS, score, 0)

    penalty = csq[0:8, :]
    for r in range(rows // 128):
        span = slice(r * 128, (r + 1) * 128)
        block_scores = acc[span, 0:128] + acc[span, 128:256] - pick_rows(penalty, bin_lanes[span, :])
        scores[:, span] = block_scores.T
        msg[2:3, span] = jnp.sum(off[span, :].T, axis=0, keepdims=True)
    local_top = jnp.max(scores[...], axis=0, keepdims=True)
    msg[0:1, :] = local_top
    msg[1:2, :] = jnp.sum(jnp.exp(scores[...] - local_top), axis=0, keepdims=True)
    msg[3:8, :] = jnp.zeros((5, rows), F32)

    def share_copy(k):
        return remote(msg, msgs.at[k], msend.at[k], mrecv.at[k], share_device((share + k) % 8))

    for k in range(1, 8):
        share_copy(k).start()
    msgs[0] = msg[...]
    for k in range(1, 8):
        share_copy(k).wait_recv()
    top = msgs[0, 0:1, :]
    for k in range(1, 8):
        top = jnp.maximum(top, msgs[k, 0:1, :])
    total = jnp.zeros_like(top)
    offset = jnp.zeros_like(top)
    for k in range(8):
        total = total + msgs[k, 1:2, :] * jnp.exp(msgs[k, 0:1, :] - top)
        offset = offset + msgs[k, 2:3, :]
    loglik[...] = top + jnp.log(total) - offset
    wt[...] = (jnp.exp(scores[...] - top) / total).astype(BF16)
    onehot = jnp.where(lax.broadcasted_iota(jnp.int32, (128, rows), 0) == bin_row[...], 1.0, 0.0).astype(BF16)
    bins = lax.dot_general(wt[...], onehot, NT, preferred_element_type=F32)
    for u in range(16):
        binsend[u] = bins[u * 8 : u * 8 + 8, :]

    def bin_copy(k):
        to = (me + k) % 16
        slot = (to % 2) * 8 + (to // 4) * 2 + (to // 2) % 2
        return remote(binsend.at[slot], binrecv.at[k], bsend.at[k], brecv.at[k], {"particle": to})

    for k in range(1, 16):
        bin_copy(k).start()

    def part_copy(c):
        return remote(
            part.at[pl.ds((1 - core) * 8, 8), :, cols(c)], sib.at[:, :, cols(c)],
            psend.at[c], precv.at[c], {"particle": sibling},
        )

    def target(t):
        return core * 8 + ((x + (1 + t) * turn) % 4) * 2

    def sum_copy(t, c):
        return remote(
            part.at[pl.ds(target(t), 2), :, cols(c)], ring.at[t, :, :, cols(c)],
            qsend.at[t, c], qrecv.at[t, c], {"particle": nxt},
        )

    def fin_copy(c):
        return remote(
            part.at[core * 8 + x * 2 + 1 - yh, :, cols(c)], fin.at[:, cols(c)],
            fsend.at[c], frecv.at[c], {"particle": partner},
        )

    sub = min(256, width)

    def second(n, _):
        @pl.when(n < CHUNKS)
        def _():
            def piece(s, _):
                at = pl.ds(pl.multiple_of(n * width + s * sub, sub), sub)
                at_im = pl.ds(pl.multiple_of(half + n * width + s * sub, sub), sub)
                re = jnp.dot(wt[...], xc[:, at], preferred_element_type=F32)
                im = jnp.dot(wt[...], xc[:, at_im], preferred_element_type=F32)
                for u in range(16):
                    span = slice(u * 8, u * 8 + 8)
                    part[u, :, at] = jnp.concatenate([re[span], im[span]], axis=0).astype(BF16)
                return 0

            lax.fori_loop(0, width // sub, piece, 0)
            part_copy(n).start()

        c = n - 1

        @pl.when((c >= 0) & (c < CHUNKS))
        def _():
            part_copy(c).wait_recv()

            def add(i, _):
                u = core * 8 + i
                part[u, :, cols(c)] = (
                    part[u, :, cols(c)].astype(F32) + sib[i, :, cols(c)].astype(F32)
                ).astype(BF16)
                return 0

            lax.fori_loop(0, 8, add, 0)
            sum_copy(0, c).start()

        for t in range(3):
            d = n - 2 - t

            @pl.when((d >= 0) & (d < CHUNKS))
            def _():
                sum_copy(t, d).wait_recv()
                for i in range(2):
                    u = target(t + 1) + i
                    part[u, :, cols(d)] = (
                        part[u, :, cols(d)].astype(F32) + ring[t, i, :, cols(d)].astype(F32)
                    ).astype(BF16)
                if t < 2:
                    sum_copy(t + 1, d).start()
                else:
                    fin_copy(d).start()

        @pl.when(n == 4)
        def _():
            whole = binsend[own]
            for k in range(1, 16):
                bin_copy(k).wait_recv()
                whole = whole + binrecv[k]
            binsum[...] = whole

        e = n - 5

        @pl.when((e >= 0) & (e < CHUNKS))
        def _():
            fin_copy(e).wait_recv()
            both = part[own, :, cols(e)].astype(F32) + fin[:, cols(e)].astype(F32)
            for h in range(2):
                at = cols(e, h * half)
                below = jnp.broadcast_to(tau[:, at], (8, width))
                for b in range(8):
                    value = ctf[b : b + 1, at]
                    below = below + binsum[:, b : b + 1] * (value * value)
                recon[:, at] = both[h * 8 : h * 8 + 8] / below

        return 0

    lax.fori_loop(0, CHUNKS + 5, second, 0)

    def finish(c, _):
        y_copy(c).wait_send()
        for t in range(3):
            ring_copy(t, c).wait_send()
            sum_copy(t, c).wait_send()
        for t in range(4):
            sib_copy(t, c).wait_send()
        part_copy(c).wait_send()
        fin_copy(c).wait_send()
        return 0

    lax.fori_loop(0, CHUNKS, finish, 0)
    for k in range(1, 8):
        share_copy(k).wait_send()
    for k in range(1, 16):
        bin_copy(k).wait_send()


def body(images, ctf_table, defocus, shifts, noise_var, tau, bank):
    rows, size = images.shape
    half = size // 2
    lane = jnp.arange(128, dtype=jnp.int32)
    turns = (shifts[:, 0:1] * (lane % 64)[None, :] + shifts[:, 1:2] * (lane // 64)[None, :]) % BOX
    angle = (2.0 * math.pi / BOX) * turns.astype(F32)
    step = jnp.broadcast_to((2.0 * math.pi / BOX) * ((2 * shifts[:, 1:2]) % BOX).astype(F32), (rows, 128))
    bin_lanes = jnp.broadcast_to(defocus[:, None], (rows, 128))
    shard = bank.reshape(8, 2, half).transpose(1, 0, 2).reshape(16, half)

    dma = pltpu.SemaphoreType.DMA
    vmem = pltpu.VMEM
    whole = pl.BlockSpec(memory_space=vmem)
    recon, loglik = pl.pallas_call(
        kernel,
        out_shape=(
            jax.ShapeDtypeStruct((8, size), F32),
            jax.ShapeDtypeStruct((1, rows), F32),
        ),
        in_specs=[pl.BlockSpec(memory_space=pl.ANY)] + [whole] * 10,
        out_specs=(whole, whole),
        scratch_shapes=[
            vmem((rows, size), BF16),
            vmem((16, 16, half), BF16),
            vmem((rows, 128), F32),
            vmem((rows, 128), F32),
            vmem((rows, 128), F32),
            vmem((rows, 256), F32),
            vmem((16, 128), F32),
            vmem((256, size // CHUNKS), BF16),
            vmem((128, size // CHUNKS), BF16),
            vmem((128, rows), F32),
            vmem((128, rows), BF16),
            vmem((8, rows), F32),
            vmem((8, 8, rows), F32),
            vmem((16, 8, 128), F32),
            vmem((16, 8, 128), F32),
            vmem((8, 128), F32),
            vmem((16, 16, half), BF16),
            vmem((8, 16, half), BF16),
            vmem((3, 2, 16, half), BF16),
            vmem((16, half), BF16),
            dma((2, CHUNKS)),
            dma,
            dma((CHUNKS,)),
            dma((CHUNKS,)),
            dma((3, CHUNKS)),
            dma((3, CHUNKS)),
            dma((4, CHUNKS)),
            dma((4, CHUNKS)),
            dma((8,)),
            dma((8,)),
            dma((16,)),
            dma((16,)),
            dma((CHUNKS,)),
            dma((CHUNKS,)),
            dma((3, CHUNKS)),
            dma((3, CHUNKS)),
            dma((CHUNKS,)),
            dma((CHUNKS,)),
        ],
        compiler_params=pltpu.CompilerParams(
            collective_id=0, has_side_effects=True, vmem_limit_bytes=60 * 1024 * 1024
        ),
        name="expectation",
    )(
        images, ctf_table, noise_var.reshape(1, size), tau.reshape(1, size), shard,
        jnp.cos(angle), jnp.sin(angle), jnp.cos(step), jnp.sin(step), bin_lanes, defocus.reshape(1, rows),
    )
    return recon.reshape(bank.shape), loglik.reshape(rows)


def solution(mesh):
    in_specs = (
        P("particle", None),
        P(),
        P("particle"),
        P("particle", None),
        P(),
        P(),
        P("classes", ("particle", "orient"), None),
    )
    out_specs = (P("classes", ("particle", "orient"), None), P("particle"))
    return jax.shard_map(body, mesh=mesh, in_specs=in_specs, out_specs=out_specs, check_vma=False)
```

```python
import jax
import jax.numpy as jnp
import numpy as np
from jax import lax
from jax.experimental import pallas as pl
from jax.experimental.pallas import tpu as pltpu
from jax.sharding import PartitionSpec as P

MESH = pl.DeviceIdType.MESH
BOX = 128
F32 = jnp.float32
BF16 = jnp.bfloat16
NT = (((1,), (1,)), ((), ()))
CHUNKS = 8
GROUP = 32


def pick_rows(table, index):
    parts = [
        jnp.take_along_axis(table, index[s : s + 8], axis=0, mode="promise_in_bounds")
        for s in range(0, index.shape[0], 8)
    ]
    return parts[0] if len(parts) == 1 else jnp.concatenate(parts, axis=0)


def kernel(
    images, ctf, noise, tau, bank, wave, moves, bin_row,
    recon, loglik,
    xc, gathered, cst, sst, rcos, rsin, bin_lanes, off, acc, csq, scaled, squared, scores, wt, msg, msgs, binsend, binrecv, binsum,
    part, sib, ring_a, ring_b, cross, fin,
    img_sem, ysend, yrecv, rsend, rrecv, ssend, srecv,
    msend, mrecv, bsend, brecv, psend, precv, qsend, arecv, brecv_ring, crecv, frecv,
):
    rows, size = xc.shape
    half = size // 2
    width = half // CHUNKS
    tiles = width // 128

    me = lax.axis_index("particle")
    cls = lax.axis_index("classes")
    ori = lax.axis_index("orient")
    core = me % 2
    yh = (me // 2) % 2
    x = me // 4
    turn = 3 + 2 * core
    nxt = (((x + 1 + 2 * core) % 4) * 2 + yh) * 2 + core
    prv = (((x + 3 + 2 * core) % 4) * 2 + yh) * 2 + core
    sibling = me + 1 - 2 * core
    partner = me + 2 - 4 * yh
    own = core * 8 + x * 2 + yh
    share = cls * 2 + ori

    def cols(c, base=0):
        return pl.ds(pl.multiple_of(base + c * width, width), width)

    def img_copy(h, c):
        where = cols(c, h * half)
        return pltpu.make_async_copy(images.at[:, where], xc.at[:, where], img_sem.at[h, c])

    def start_images(c, _):
        img_copy(0, c).start()
        img_copy(1, c).start()
        return 0

    lax.fori_loop(0, CHUNKS, start_images, 0)

    def share_device(s):
        return {"classes": s // 2, "orient": s % 2}

    def arrange(c, _):
        pieces = [bank[k, :, cols(c, h * half)].astype(F32) for h in range(2) for k in range(2)]
        gathered[own, :, cols(c)] = jnp.concatenate(pieces, axis=0).astype(BF16)
        return 0

    lax.fori_loop(0, CHUNKS, arrange, 0)

    barrier = pltpu.get_barrier_semaphore()
    for k in range(1, 16):
        pl.semaphore_signal(barrier, inc=1, device_id={"particle": (me + k) % 16}, device_id_type=MESH)
    for k in range(1, 8):
        pl.semaphore_signal(barrier, inc=1, device_id=share_device((share + k) % 8), device_id_type=MESH)
    pl.semaphore_wait(barrier, 22)

    def remote(src, dst, send, recv, to):
        return pltpu.make_async_remote_copy(
            src_ref=src, dst_ref=dst, send_sem=send, recv_sem=recv, device_id=to, device_id_type=MESH
        )

    def y_copy(c, q=None):
        q = cols(c) if q is None else q
        return remote(
            gathered.at[own, :, q], gathered.at[own, :, q], ysend, yrecv.at[c], {"particle": partner}
        )

    def pair(t, q):
        return gathered.at[pl.ds(core * 8 + ((x + t * turn) % 4) * 2, 2), :, q]

    def ring_copy(t, c, q=None):
        q = cols(c) if q is None else q
        return remote(pair(t, q), pair(t, q), rsend.at[t], rrecv.at[t, c], {"particle": nxt})

    def sib_copy(t, c, q=None):
        q = cols(c) if q is None else q
        return remote(pair(t, q), pair(t, q), ssend.at[t], srecv.at[t, c], {"particle": sibling})

    def start_y(c, _):
        y_copy(c).start()
        return 0

    lax.fori_loop(0, CHUNKS, start_y, 0)

    lane = lax.broadcasted_iota(jnp.int32, (128, 128), 1)

    waves = jnp.broadcast_to(wave[...], (8, BOX))

    def look(turns):
        turns = turns & (BOX - 1)
        return jnp.concatenate(
            [
                jnp.take_along_axis(waves, turns[s : s + 8], axis=1, mode="promise_in_bounds")
                for s in range(0, 128, 8)
            ],
            axis=0,
        )

    def phases(r, _):
        span = pl.ds(pl.multiple_of(r * 128, 128), 128)
        shift_x, shift_y, bins_of = [
            jnp.broadcast_to(row.astype(F32), (128, 128)).T.astype(jnp.int32)
            for row in (moves[0:1, span], moves[1:2, span], bin_row[:, span])
        ]
        turns = shift_x * (lane % 64) + shift_y * (lane // 64)
        cst[span, :] = look(turns)
        sst[span, :] = look(turns - BOX // 4)
        rcos[span, :] = look(2 * shift_y)
        rsin[span, :] = look(2 * shift_y - BOX // 4)
        bin_lanes[span, :] = bins_of
        return 0

    lax.fori_loop(0, rows // 128, phases, 0)
    off[...] = jnp.zeros_like(off)
    acc[...] = jnp.zeros_like(acc)
    csq[...] = jnp.zeros_like(csq)

    def shift_chunk(c, part_of, with_offset):
        lows = [pl.multiple_of(c * width + j * 128, 128) for j in range(tiles)]

        def group(g, _):
            where = pl.ds(pl.multiple_of(g * GROUP, GROUP), GROUP)
            cosine, sine = cst[where, :], sst[where, :]
            step_c, step_s = rcos[where, :], rsin[where, :]
            index = bin_lanes[where, :]
            total = off[where, :] if with_offset else None
            for low in lows:
                at_re = pl.ds(low, 128)
                at_im = pl.ds(pl.multiple_of(half + low, 128), 128)
                re = xc[where, at_re].astype(F32)
                im = xc[where, at_im].astype(F32)
                out_re = re * cosine - im * sine
                out_im = re * sine + im * cosine
                if with_offset:
                    total = total + out_re * out_re * (0.5 / noise[:, at_re])
                    total = total + out_im * out_im * (0.5 / noise[:, at_im])
                xc[where, at_re] = (out_re * pick_rows(ctf[:, at_re], index)).astype(BF16)
                xc[where, at_im] = (out_im * pick_rows(ctf[:, at_im], index)).astype(BF16)
                cosine, sine = cosine * step_c - sine * step_s, sine * step_c + cosine * step_s
            cst[where, :] = cosine
            sst[where, :] = sine
            if with_offset:
                off[where, :] = total
            return 0

        per = rows // GROUP // 2
        lax.fori_loop(part_of * per, part_of * per + per, group, 0)

    def score(c):
        for t in range(4):
            sib_copy(t, c).wait_recv()
        for h in range(2):
            at = cols(c, h * half)
            inverse = 1.0 / noise[:, at]

            def prepare(m, _):
                b0 = gathered[2 * m, :, cols(c)].astype(F32)
                b1 = gathered[2 * m + 1, :, cols(c)].astype(F32)
                b = jnp.concatenate([b0[h * 8 : h * 8 + 8], b1[h * 8 : h * 8 + 8]], axis=0)
                value = b * inverse
                high = value.astype(BF16)
                to = pl.multiple_of(m * 16, 16)
                scaled[pl.ds(to, 16), h * width : (h + 1) * width] = high
                scaled[pl.ds(128 + to, 16), h * width : (h + 1) * width] = (value - high.astype(F32)).astype(BF16)
                squared[pl.ds(to, 16), h * width : (h + 1) * width] = (b * b).astype(BF16)
                return 0

            lax.fori_loop(0, 8, prepare, 0)
            table = ctf[:, at]
            cs = 0.5 * table * table * inverse
            cs = jnp.concatenate([cs, cs], axis=0).astype(BF16)
            csq[...] += lax.dot_general(
                cs, squared[:, h * width : (h + 1) * width], NT, preferred_element_type=F32
            )

        def block(r, _):
            where = pl.ds(pl.multiple_of(r * 384, 384), 384)
            acc[where, :] += lax.dot_general(
                xc[where, cols(c)], scaled[:, :width], NT, preferred_element_type=F32
            ) + lax.dot_general(xc[where, cols(c, half)], scaled[:, width:], NT, preferred_element_type=F32)
            return 0

        lax.fori_loop(0, rows // 384, block, 0)

    def first(n, _):
        @pl.when(n < CHUNKS)
        def _():
            y_copy(n).wait_recv()
            ring_copy(0, n).start()
            sib_copy(0, n).start()

        for t in range(1, 4):
            c = n - 2 * t

            @pl.when((c >= 0) & (c < CHUNKS))
            def _():
                ring_copy(t - 1, c).wait_recv()
                if t < 3:
                    ring_copy(t, c).start()
                sib_copy(t, c).start()

        c = n // 2
        part_of = n % 2

        @pl.when(part_of == 0)
        def _():
            img_copy(0, c).wait()
            img_copy(1, c).wait()

        @pl.when(c == share)
        def _():
            shift_chunk(c, part_of, True)

        @pl.when(c != share)
        def _():
            shift_chunk(c, part_of, False)

        @pl.when(n >= CHUNKS)
        def _():
            score(n - CHUNKS)

        return 0

    lax.fori_loop(0, 2 * CHUNKS, first, 0)


    penalty = csq[0:8, :]
    for r in range(rows // 128):
        span = slice(r * 128, (r + 1) * 128)
        block_scores = acc[span, 0:128] + acc[span, 128:256] - pick_rows(penalty, bin_lanes[span, :])
        scores[:, span] = block_scores.T
        msg[2:3, span] = jnp.sum(off[span, :].T, axis=0, keepdims=True)
    local_top = jnp.max(scores[...], axis=0, keepdims=True)
    msg[0:1, :] = local_top
    msg[1:2, :] = jnp.sum(jnp.exp(scores[...] - local_top), axis=0, keepdims=True)
    msg[3:8, :] = jnp.zeros((5, rows), F32)

    def share_copy(k):
        return remote(msg, msgs.at[k], msend.at[k], mrecv.at[k], share_device((share + k) % 8))

    for k in range(1, 8):
        share_copy(k).start()
    msgs[0] = msg[...]
    for k in range(1, 8):
        share_copy(k).wait_recv()
    top = msgs[0, 0:1, :]
    for k in range(1, 8):
        top = jnp.maximum(top, msgs[k, 0:1, :])
    total = jnp.zeros_like(top)
    offset = jnp.zeros_like(top)
    for k in range(8):
        total = total + msgs[k, 1:2, :] * jnp.exp(msgs[k, 0:1, :] - top)
        offset = offset + msgs[k, 2:3, :]
    loglik[...] = top + jnp.log(total) - offset
    wt[...] = (jnp.exp(scores[...] - top) / total).astype(BF16)
    onehot = jnp.where(lax.broadcasted_iota(jnp.int32, (128, rows), 0) == bin_row[...], 1.0, 0.0).astype(BF16)
    bins = lax.dot_general(wt[...], onehot, NT, preferred_element_type=F32)
    for u in range(16):
        binsend[u] = bins[u * 8 : u * 8 + 8, :]

    def bin_copy(k):
        to = (me + k) % 16
        slot = (to % 2) * 8 + (to // 4) * 2 + (to // 2) % 2
        return remote(binsend.at[slot], binrecv.at[k], bsend.at[k], brecv.at[k], {"particle": to})

    for k in range(1, 16):
        bin_copy(k).start()

    steps = CHUNKS
    middle = half // 2
    span_of = middle // steps
    sub = min(256, span_of)

    def at_step(route, d):
        return pl.ds(pl.multiple_of(route * middle + d * span_of, span_of), span_of)

    def local(d):
        return pl.ds(pl.multiple_of(d * span_of, span_of), span_of)

    def everything(route):
        return pl.ds(route * middle, middle)

    def target(t):
        return (x + (1 + t) * turn) % 4

    def part_copy(route, d, q=None):
        q = at_step(route, d) if q is None else q
        return remote(
            part.at[1 - core, :, :, :, q], sib.at[:, :, :, q],
            psend.at[route], precv.at[route, d], {"particle": sibling},
        )

    def ring_a_copy(t, d, q=None):
        p = local(d) if q is None else q
        q = at_step(0, d) if q is None else q
        return remote(
            part.at[core, target(t), :, :, q], ring_a.at[t, :, :, p],
            qsend.at[t], arecv.at[t, d], {"particle": nxt},
        )

    def fin_copy(d, q=None):
        p = local(d) if q is None else q
        q = at_step(0, d) if q is None else q
        return remote(
            part.at[core, x, 1 - yh, :, q], fin.at[:, p], qsend.at[3], frecv.at[d], {"particle": partner}
        )

    def cross_copy(d, whole=False):
        p = everything(0) if whole else local(d)
        q = everything(1) if whole else at_step(1, d)
        return remote(
            part.at[core, :, 1 - yh, :, q], cross.at[:, :, p], qsend.at[4], crecv.at[d], {"particle": partner}
        )

    def ring_b_copy(t, d, whole=False):
        p = everything(0) if whole else local(d)
        q = everything(1) if whole else at_step(1, d)
        return remote(
            part.at[core, target(t), yh, :, q], ring_b.at[t, :, p],
            qsend.at[5 + t], brecv_ring.at[t, d], {"particle": nxt},
        )

    def gain(i, j, q, other):
        part[core, i, j, :, q] = (part[core, i, j, :, q].astype(F32) + other.astype(F32)).astype(BF16)

    def result(route, d, other):
        q = at_step(route, d)
        both = part[core, x, yh, :, q].astype(F32) + other.astype(F32)
        for h in range(2):
            at = pl.ds(pl.multiple_of(h * half + route * middle + d * span_of, span_of), span_of)
            below = jnp.broadcast_to(tau[:, at], (8, span_of))
            for b in range(8):
                value = ctf[b : b + 1, at]
                below = below + binsum[:, b : b + 1] * (value * value)
            value = both[h * 8 : h * 8 + 8] / below
            recon[0, :, at] = value[0:4]
            recon[1, :, at] = value[4:8]

    def stage(n, lag):
        d = n - lag
        return d, pl.when((d >= 0) & (d < steps))

    def second(n, _):
        @pl.when(n < steps)
        def _():
            per = span_of // sub

            def piece(s, _):
                low = (s // per) * middle + n * span_of + (s % per) * sub
                at = pl.ds(pl.multiple_of(low, sub), sub)
                at_im = pl.ds(pl.multiple_of(half + low, sub), sub)
                re = jnp.dot(wt[...], xc[:, at], preferred_element_type=F32)
                im = jnp.dot(wt[...], xc[:, at_im], preferred_element_type=F32)
                for u in range(16):
                    span = slice(u * 8, u * 8 + 8)
                    part[u // 8, (u // 2) % 4, u % 2, :, at] = jnp.concatenate(
                        [re[span], im[span]], axis=0
                    ).astype(BF16)
                return 0

            lax.fori_loop(0, 2 * per, piece, 0)
            part_copy(0, n).start()
            part_copy(1, n).start()

        d1, on1 = stage(n, 1)

        @on1
        def _():
            for route in range(2):
                part_copy(route, d1).wait_recv()
                q = at_step(route, d1)

                def add(i, _):
                    for j in range(2):
                        gain(i, j, q, sib[i, j, :, q])
                    return 0

                lax.fori_loop(0, 4, add, 0)
                if route == 0:
                    ring_a_copy(0, d1).start()
                else:
                    cross_copy(d1).start()

        d2, on2 = stage(n, 3)

        @on2
        def _():
            ring_a_copy(0, d2).wait_recv()
            for j in range(2):
                gain(target(1), j, at_step(0, d2), ring_a[0, j, :, local(d2)])
            ring_a_copy(1, d2).start()
            cross_copy(d2).wait_recv()
            for i in range(4):
                gain(i, yh, at_step(1, d2), cross[i, :, local(d2)])
            ring_b_copy(0, d2).start()

        d3, on3 = stage(n, 5)

        @on3
        def _():
            ring_a_copy(1, d3).wait_recv()
            for j in range(2):
                gain(target(2), j, at_step(0, d3), ring_a[1, j, :, local(d3)])
            ring_a_copy(2, d3).start()
            ring_b_copy(0, d3).wait_recv()
            gain(target(1), yh, at_step(1, d3), ring_b[0, :, local(d3)])
            ring_b_copy(1, d3).start()

        d4, on4 = stage(n, 7)

        @on4
        def _():
            ring_a_copy(2, d4).wait_recv()
            for j in range(2):
                gain(x, j, at_step(0, d4), ring_a[2, j, :, local(d4)])
            fin_copy(d4).start()
            ring_b_copy(1, d4).wait_recv()
            gain(target(2), yh, at_step(1, d4), ring_b[1, :, local(d4)])
            ring_b_copy(2, d4).start()

        @pl.when(n == 5)
        def _():
            whole = binsend[own]
            for k in range(1, 16):
                bin_copy(k).wait_recv()
                whole = whole + binrecv[k]
            binsum[...] = whole

        d5, on5 = stage(n, 9)

        @on5
        def _():
            fin_copy(d5).wait_recv()
            result(0, d5, fin[:, local(d5)])
            ring_b_copy(2, d5).wait_recv()
            result(1, d5, ring_b[2, :, local(d5)])

        return 0

    lax.fori_loop(0, steps + 9, second, 0)

    full = pl.ds(0, half)
    y_copy(0, full).wait_send()
    for t in range(3):
        ring_copy(t, 0, full).wait_send()
        ring_a_copy(t, 0, everything(0)).wait_send()
        ring_b_copy(t, 0, True).wait_send()
    for t in range(4):
        sib_copy(t, 0, full).wait_send()
    for route in range(2):
        part_copy(route, 0, everything(route)).wait_send()
    fin_copy(0, everything(0)).wait_send()
    cross_copy(0, True).wait_send()
    for k in range(1, 8):
        share_copy(k).wait_send()
    for k in range(1, 16):
        bin_copy(k).wait_send()


def body(images, ctf_table, defocus, shifts, noise_var, tau, bank):
    rows, size = images.shape
    half = size // 2
    wave = np.cos(2.0 * np.pi / BOX * np.arange(BOX)).astype(np.float32)
    wave = jnp.asarray(wave[None, :])

    dma = pltpu.SemaphoreType.DMA
    vmem = pltpu.VMEM
    whole = pl.BlockSpec(memory_space=vmem)
    recon, loglik = pl.pallas_call(
        kernel,
        out_shape=(
            jax.ShapeDtypeStruct(bank.shape, F32),
            jax.ShapeDtypeStruct((1, rows), F32),
        ),
        in_specs=[pl.BlockSpec(memory_space=pl.ANY)] + [whole] * 7,
        out_specs=(whole, whole),
        scratch_shapes=[
            vmem((rows, size), BF16),
            vmem((16, 16, half), BF16),
            vmem((rows, 128), F32),
            vmem((rows, 128), F32),
            vmem((rows, 128), F32),
            vmem((rows, 128), F32),
            vmem((rows, 128), jnp.int32),
            vmem((rows, 128), F32),
            vmem((rows, 256), F32),
            vmem((16, 128), F32),
            vmem((256, size // CHUNKS), BF16),
            vmem((128, size // CHUNKS), BF16),
            vmem((128, rows), F32),
            vmem((128, rows), BF16),
            vmem((8, rows), F32),
            vmem((8, 8, rows), F32),
            vmem((16, 8, 128), F32),
            vmem((16, 8, 128), F32),
            vmem((8, 128), F32),
            vmem((2, 4, 2, 16, half), BF16),
            vmem((4, 2, 16, half), BF16),
            vmem((3, 2, 16, half // 2), BF16),
            vmem((3, 16, half // 2), BF16),
            vmem((4, 16, half // 2), BF16),
            vmem((16, half // 2), BF16),
            dma((2, CHUNKS)),
            dma,
            dma((CHUNKS,)),
            dma((3,)),
            dma((3, CHUNKS)),
            dma((4,)),
            dma((4, CHUNKS)),
            dma((8,)),
            dma((8,)),
            dma((16,)),
            dma((16,)),
            dma((2,)),
            dma((2, CHUNKS)),
            dma((8,)),
            dma((3, CHUNKS)),
            dma((3, CHUNKS)),
            dma((CHUNKS,)),
            dma((CHUNKS,)),
        ],
        compiler_params=pltpu.CompilerParams(
            collective_id=0, has_side_effects=True, vmem_limit_bytes=60 * 1024 * 1024
        ),
        name="expectation",
    )(
        images, ctf_table, noise_var.reshape(1, size), tau.reshape(1, size), bank, wave,
        shifts.T, defocus[None, :],
    )
    return recon, loglik.reshape(rows)


def solution(mesh):
    in_specs = (
        P("particle", None),
        P(),
        P("particle"),
        P("particle", None),
        P(),
        P(),
        P("classes", ("particle", "orient"), None),
    )
    out_specs = (P("classes", ("particle", "orient"), None), P("particle"))
    return jax.shard_map(body, mesh=mesh, in_specs=in_specs, out_specs=out_specs, check_vma=False)
```

```python
import jax
import jax.numpy as jnp
import numpy as np
from jax import lax
from jax.experimental import pallas as pl
from jax.experimental.pallas import tpu as pltpu
from jax.sharding import PartitionSpec as P

MESH = pl.DeviceIdType.MESH
BOX = 128
F32 = jnp.float32
BF16 = jnp.bfloat16
NT = (((1,), (1,)), ((), ()))
CHUNKS = 8
GROUP = 32
LAG = 3
SCORE_ROWS = 768


def pick_rows(table, index):
    parts = [
        jnp.take_along_axis(table, index[s : s + 8], axis=0, mode="promise_in_bounds")
        for s in range(0, index.shape[0], 8)
    ]
    return parts[0] if len(parts) == 1 else jnp.concatenate(parts, axis=0)


def kernel(
    images, ctf, noise, tau, bank, wave, moves, bin_row,
    recon, loglik,
    xc, gathered, cst, sst, rcos, rsin, bin_lanes, off, acc, csq, scaled, squared, scores, wt, msg, msgs, binsend, binrecv, binsum,
    part, sib, ring_a, ring_b, cross, fin,
    img_sem, ysend, yrecv, rsend, rrecv, ssend, srecv,
    msend, mrecv, bsend, brecv, psend, precv, qsend, arecv, brecv_ring, crecv, frecv,
):
    rows, size = xc.shape
    half = size // 2
    width = half // CHUNKS
    tiles = width // 128

    me = lax.axis_index("particle")
    cls = lax.axis_index("classes")
    ori = lax.axis_index("orient")
    core = me % 2
    yh = (me // 2) % 2
    x = me // 4
    turn = 3 + 2 * core
    nxt = (((x + 1 + 2 * core) % 4) * 2 + yh) * 2 + core
    prv = (((x + 3 + 2 * core) % 4) * 2 + yh) * 2 + core
    sibling = me + 1 - 2 * core
    partner = me + 2 - 4 * yh
    own = core * 8 + x * 2 + yh
    share = cls * 2 + ori

    def cols(c, base=0):
        return pl.ds(pl.multiple_of(base + c * width, width), width)

    def img_copy(h, c):
        where = cols(c, h * half)
        return pltpu.make_async_copy(images.at[:, where], xc.at[:, where], img_sem.at[h, c])

    def start_images(c, _):
        img_copy(0, c).start()
        img_copy(1, c).start()
        return 0

    lax.fori_loop(0, 2, start_images, 0)

    def share_device(s):
        return {"classes": s // 2, "orient": s % 2}

    def arrange(c, _):
        pieces = [bank[k, :, cols(c, h * half)].astype(F32) for h in range(2) for k in range(2)]
        gathered[own, :, cols(c)] = jnp.concatenate(pieces, axis=0).astype(BF16)
        return 0

    lax.fori_loop(0, CHUNKS, arrange, 0)

    barrier = pltpu.get_barrier_semaphore()
    for k in range(1, 16):
        pl.semaphore_signal(barrier, inc=1, device_id={"particle": (me + k) % 16}, device_id_type=MESH)
    for k in range(1, 8):
        pl.semaphore_signal(barrier, inc=1, device_id=share_device((share + k) % 8), device_id_type=MESH)
    pl.semaphore_wait(barrier, 22)

    def remote(src, dst, send, recv, to):
        return pltpu.make_async_remote_copy(
            src_ref=src, dst_ref=dst, send_sem=send, recv_sem=recv, device_id=to, device_id_type=MESH
        )

    def y_copy(c, q=None):
        q = cols(c) if q is None else q
        return remote(
            gathered.at[own, :, q], gathered.at[own, :, q], ysend, yrecv.at[c], {"particle": partner}
        )

    def pair(t, q):
        return gathered.at[pl.ds(core * 8 + ((x + t * turn) % 4) * 2, 2), :, q]

    def ring_copy(t, c, q=None):
        q = cols(c) if q is None else q
        block = pair(1 if t == 2 else 0, q)
        return remote(block, block, rsend.at[t], rrecv.at[t, c], {"particle": prv if t == 1 else nxt})

    def sib_copy(t, c, q=None):
        q = cols(c) if q is None else q
        return remote(pair(t, q), pair(t, q), ssend.at[t], srecv.at[t, c], {"particle": sibling})

    def start_y(c, _):
        y_copy(c).start()
        return 0

    lax.fori_loop(0, CHUNKS, start_y, 0)

    lane = lax.broadcasted_iota(jnp.int32, (128, 128), 1)

    waves = jnp.broadcast_to(wave[...], (8, BOX))

    def look(turns):
        turns = turns & (BOX - 1)
        return jnp.concatenate(
            [
                jnp.take_along_axis(waves, turns[s : s + 8], axis=1, mode="promise_in_bounds")
                for s in range(0, 128, 8)
            ],
            axis=0,
        )

    def phases(r, _):
        span = pl.ds(pl.multiple_of(r * 128, 128), 128)
        shift_x, shift_y, bins_of = [
            jnp.broadcast_to(row.astype(F32), (128, 128)).T.astype(jnp.int32)
            for row in (moves[0:1, span], moves[1:2, span], bin_row[span].reshape(1, 128))
        ]
        turns = shift_x * (lane % 64) + shift_y * (lane // 64)
        cst[span, :] = look(turns)
        sst[span, :] = look(turns - BOX // 4)
        rcos[span, :] = look(2 * shift_y)
        rsin[span, :] = look(2 * shift_y - BOX // 4)
        bin_lanes[span, :] = bins_of
        return 0

    lax.fori_loop(0, rows // 128, phases, 0)
    off[...] = jnp.zeros_like(off)
    acc[...] = jnp.zeros_like(acc)
    csq[...] = jnp.zeros_like(csq)

    def shift_chunk(c, part_of, with_offset):
        lows = [pl.multiple_of(c * width + j * 128, 128) for j in range(tiles)]

        def group(g, _):
            where = pl.ds(pl.multiple_of(g * GROUP, GROUP), GROUP)
            cosine, sine = cst[where, :], sst[where, :]
            step_c, step_s = rcos[where, :], rsin[where, :]
            index = bin_lanes[where, :]
            total = off[where, :] if with_offset else None
            for low in lows:
                at_re = pl.ds(low, 128)
                at_im = pl.ds(pl.multiple_of(half + low, 128), 128)
                re = xc[where, at_re].astype(F32)
                im = xc[where, at_im].astype(F32)
                out_re = re * cosine - im * sine
                out_im = re * sine + im * cosine
                if with_offset:
                    total = total + out_re * out_re * (0.5 / noise[:, at_re])
                    total = total + out_im * out_im * (0.5 / noise[:, at_im])
                xc[where, at_re] = (out_re * pick_rows(ctf[:, at_re], index)).astype(BF16)
                xc[where, at_im] = (out_im * pick_rows(ctf[:, at_im], index)).astype(BF16)
                cosine, sine = cosine * step_c - sine * step_s, sine * step_c + cosine * step_s
            cst[where, :] = cosine
            sst[where, :] = sine
            if with_offset:
                off[where, :] = total
            return 0

        per = rows // GROUP // 2
        lax.fori_loop(part_of * per, part_of * per + per, group, 0)

    def score(c):
        for t in range(4):
            sib_copy(t, c).wait_recv()
        for h in range(2):
            at = cols(c, h * half)
            inverse = 1.0 / noise[:, at]

            def prepare(m, _):
                b0 = gathered[2 * m, :, cols(c)].astype(F32)
                b1 = gathered[2 * m + 1, :, cols(c)].astype(F32)
                b = jnp.concatenate([b0[h * 8 : h * 8 + 8], b1[h * 8 : h * 8 + 8]], axis=0)
                value = b * inverse
                high = value.astype(BF16)
                to = pl.multiple_of(m * 16, 16)
                scaled[pl.ds(to, 16), h * width : (h + 1) * width] = high
                scaled[pl.ds(128 + to, 16), h * width : (h + 1) * width] = (value - high.astype(F32)).astype(BF16)
                squared[pl.ds(to, 16), h * width : (h + 1) * width] = (b * b).astype(BF16)
                return 0

            lax.fori_loop(0, 8, prepare, 0)
            table = ctf[:, at]
            cs = 0.5 * table * table * inverse
            cs = jnp.concatenate([cs, cs], axis=0).astype(BF16)
            csq[...] += lax.dot_general(
                cs, squared[:, h * width : (h + 1) * width], NT, preferred_element_type=F32
            )

        def block(r, _):
            where = pl.ds(pl.multiple_of(r * SCORE_ROWS, SCORE_ROWS), SCORE_ROWS)
            acc[where, :] += lax.dot_general(
                xc[where, cols(c)], scaled[:, :width], NT, preferred_element_type=F32
            ) + lax.dot_general(xc[where, cols(c, half)], scaled[:, width:], NT, preferred_element_type=F32)
            return 0

        lax.fori_loop(0, rows // SCORE_ROWS, block, 0)

    def first(n, _):
        @pl.when(n < CHUNKS)
        def _():
            y_copy(n).wait_recv()
            ring_copy(0, n).start()
            ring_copy(1, n).start()
            sib_copy(0, n).start()

        near = n - LAG

        @pl.when((near >= 0) & (near < CHUNKS))
        def _():
            ring_copy(0, near).wait_recv()
            ring_copy(2, near).start()
            sib_copy(1, near).start()
            ring_copy(1, near).wait_recv()
            sib_copy(3, near).start()

        far = n - 2 * LAG

        @pl.when((far >= 0) & (far < CHUNKS))
        def _():
            ring_copy(2, far).wait_recv()
            sib_copy(2, far).start()

        c = n // 2
        part_of = n % 2
        shifting = n < 2 * CHUNKS

        @pl.when(shifting & (part_of == 0))
        def _():
            @pl.when(c + 2 < CHUNKS)
            def _():
                start_images(c + 2, 0)

            img_copy(0, c).wait()
            img_copy(1, c).wait()

        @pl.when(shifting & (c == share))
        def _():
            shift_chunk(c, part_of, True)

        @pl.when(shifting & (c != share))
        def _():
            shift_chunk(c, part_of, False)

        ready = n - 2 * LAG - 2

        @pl.when((ready >= 0) & (ready < CHUNKS))
        def _():
            score(ready)

        return 0

    lax.fori_loop(0, max(2 * LAG + 2 + CHUNKS, 2 * CHUNKS), first, 0)

    penalty = csq[0:8, :]
    for r in range(rows // 128):
        span = slice(r * 128, (r + 1) * 128)
        block_scores = acc[span, 0:128] + acc[span, 128:256] - pick_rows(penalty, bin_lanes[span, :])
        scores[:, span] = block_scores.T
        msg[2:3, span] = jnp.sum(off[span, :].T, axis=0, keepdims=True)
    local_top = jnp.max(scores[...], axis=0, keepdims=True)
    msg[0:1, :] = local_top
    msg[1:2, :] = jnp.sum(jnp.exp(scores[...] - local_top), axis=0, keepdims=True)
    msg[3:8, :] = jnp.zeros((5, rows), F32)

    def share_copy(k):
        return remote(msg, msgs.at[k], msend.at[k], mrecv.at[k], share_device((share + k) % 8))

    for k in range(1, 8):
        share_copy(k).start()
    msgs[0] = msg[...]
    for k in range(1, 8):
        share_copy(k).wait_recv()
    top = msgs[0, 0:1, :]
    for k in range(1, 8):
        top = jnp.maximum(top, msgs[k, 0:1, :])
    total = jnp.zeros_like(top)
    offset = jnp.zeros_like(top)
    for k in range(8):
        total = total + msgs[k, 1:2, :] * jnp.exp(msgs[k, 0:1, :] - top)
        offset = offset + msgs[k, 2:3, :]
    loglik[...] = (top + jnp.log(total) - offset).reshape(rows)
    wt[...] = (jnp.exp(scores[...] - top) / total).astype(BF16)
    onehot = jnp.where(lax.broadcasted_iota(jnp.int32, (128, rows), 0) == bin_row[...].reshape(1, rows), 1.0, 0.0).astype(BF16)
    bins = lax.dot_general(wt[...], onehot, NT, preferred_element_type=F32)
    for u in range(16):
        binsend[u] = bins[u * 8 : u * 8 + 8, :]

    def bin_copy(k):
        to = (me + k) % 16
        slot = (to % 2) * 8 + (to // 4) * 2 + (to // 2) % 2
        return remote(binsend.at[slot], binrecv.at[k], bsend.at[k], brecv.at[k], {"particle": to})

    for k in range(1, 16):
        bin_copy(k).start()

    steps = CHUNKS
    middle = half // 2
    span_of = middle // steps
    sub = min(256, span_of)

    def at_step(route, d):
        return pl.ds(pl.multiple_of(route * middle + d * span_of, span_of), span_of)

    def local(d):
        return pl.ds(pl.multiple_of(d * span_of, span_of), span_of)

    def everything(route):
        return pl.ds(route * middle, middle)

    def part_copy(route, d, q=None):
        q = at_step(route, d) if q is None else q
        return remote(
            part.at[1 - core, :, :, :, q], sib.at[:, :, :, q],
            psend.at[route], precv.at[route, d], {"particle": sibling},
        )

    onward, across, behind = (x + 3 * turn) % 4, (x + 2) % 4, (x + turn) % 4
    goal = (across, behind, onward)
    to = (nxt, prv, nxt)

    def ring_a_copy(t, d, q=None):
        p = local(d) if q is None else q
        q = at_step(0, d) if q is None else q
        return remote(
            part.at[core, goal[t], :, :, q], ring_a.at[t, :, :, p],
            qsend.at[t], arecv.at[t, d], {"particle": to[t]},
        )

    def fin_copy(d, q=None):
        p = local(d) if q is None else q
        q = at_step(0, d) if q is None else q
        return remote(
            part.at[core, x, 1 - yh, :, q], fin.at[:, p], qsend.at[3], frecv.at[d], {"particle": partner}
        )

    def cross_copy(d, whole=False):
        p = everything(0) if whole else local(d)
        q = everything(1) if whole else at_step(1, d)
        return remote(
            part.at[core, :, 1 - yh, :, q], cross.at[:, :, p], qsend.at[4], crecv.at[d], {"particle": partner}
        )

    def ring_b_copy(t, d, whole=False):
        p = everything(0) if whole else local(d)
        q = everything(1) if whole else at_step(1, d)
        return remote(
            part.at[core, goal[t], yh, :, q], ring_b.at[t, :, p],
            qsend.at[5 + t], brecv_ring.at[t, d], {"particle": to[t]},
        )

    def gain(i, j, q, *others):
        value = part[core, i, j, :, q].astype(F32)
        for other in others:
            value = value + other.astype(F32)
        part[core, i, j, :, q] = value.astype(BF16)

    def result(route, d, *others):
        q = at_step(route, d)
        both = part[core, x, yh, :, q].astype(F32)
        for other in others:
            both = both + other.astype(F32)
        for h in range(2):
            at = pl.ds(pl.multiple_of(h * half + route * middle + d * span_of, span_of), span_of)
            below = jnp.broadcast_to(tau[:, at], (8, span_of))
            for b in range(8):
                value = ctf[b : b + 1, at]
                below = below + binsum[:, b : b + 1] * (value * value)
            value = both[h * 8 : h * 8 + 8] / below
            recon[0, :, at] = value[0:4]
            recon[1, :, at] = value[4:8]

    def stage(n, lag):
        d = n - lag
        return d, pl.when((d >= 0) & (d < steps))

    def second(n, _):
        @pl.when(n < steps)
        def _():
            per = span_of // sub

            def piece(s, _):
                low = (s // per) * middle + n * span_of + (s % per) * sub
                at = pl.ds(pl.multiple_of(low, sub), sub)
                at_im = pl.ds(pl.multiple_of(half + low, sub), sub)
                re = jnp.dot(wt[...], xc[:, at], preferred_element_type=F32)
                im = jnp.dot(wt[...], xc[:, at_im], preferred_element_type=F32)
                for u in range(16):
                    span = slice(u * 8, u * 8 + 8)
                    part[u // 8, (u // 2) % 4, u % 2, :, at] = jnp.concatenate(
                        [re[span], im[span]], axis=0
                    ).astype(BF16)
                return 0

            lax.fori_loop(0, 2 * per, piece, 0)
            part_copy(0, n).start()
            part_copy(1, n).start()

        d1, on1 = stage(n, 1)

        @on1
        def _():
            for route in range(2):
                part_copy(route, d1).wait_recv()
                q = at_step(route, d1)

                def add(i, _):
                    for j in range(2):
                        gain(i, j, q, sib[i, j, :, q])
                    return 0

                lax.fori_loop(0, 4, add, 0)
                if route == 0:
                    ring_a_copy(0, d1).start()
                    ring_a_copy(1, d1).start()
                else:
                    cross_copy(d1).start()

        d2, on2 = stage(n, 3)

        @on2
        def _():
            ring_a_copy(0, d2).wait_recv()
            for j in range(2):
                gain(onward, j, at_step(0, d2), ring_a[0, j, :, local(d2)])
            ring_a_copy(2, d2).start()
            cross_copy(d2).wait_recv()
            for i in range(4):
                gain(i, yh, at_step(1, d2), cross[i, :, local(d2)])
            ring_b_copy(0, d2).start()
            ring_b_copy(1, d2).start()

        d3, on3 = stage(n, 5)

        @on3
        def _():
            ring_b_copy(0, d3).wait_recv()
            gain(onward, yh, at_step(1, d3), ring_b[0, :, local(d3)])
            ring_b_copy(2, d3).start()
            ring_a_copy(1, d3).wait_recv()
            ring_a_copy(2, d3).wait_recv()
            for j in range(2):
                gain(x, j, at_step(0, d3), ring_a[1, j, :, local(d3)], ring_a[2, j, :, local(d3)])
            fin_copy(d3).start()

        @pl.when(n == 5)
        def _():
            whole = binsend[own]
            for k in range(1, 16):
                bin_copy(k).wait_recv()
                whole = whole + binrecv[k]
            binsum[...] = whole

        d4, on4 = stage(n, 7)

        @on4
        def _():
            fin_copy(d4).wait_recv()
            result(0, d4, fin[:, local(d4)])
            ring_b_copy(1, d4).wait_recv()
            ring_b_copy(2, d4).wait_recv()
            result(1, d4, ring_b[1, :, local(d4)], ring_b[2, :, local(d4)])

        return 0

    lax.fori_loop(0, steps + 7, second, 0)

    full = pl.ds(0, half)
    y_copy(0, full).wait_send()
    for t in range(3):
        ring_copy(t, 0, full).wait_send()
        ring_a_copy(t, 0, everything(0)).wait_send()
        ring_b_copy(t, 0, True).wait_send()
    for t in range(4):
        sib_copy(t, 0, full).wait_send()
    for route in range(2):
        part_copy(route, 0, everything(route)).wait_send()
    fin_copy(0, everything(0)).wait_send()
    cross_copy(0, True).wait_send()
    for k in range(1, 8):
        share_copy(k).wait_send()
    for k in range(1, 16):
        bin_copy(k).wait_send()


def body(images, ctf_table, defocus, shifts, noise_var, tau, bank):
    rows, size = images.shape
    half = size // 2
    wave = np.cos(2.0 * np.pi / BOX * np.arange(BOX)).astype(np.float32)
    wave = jnp.asarray(wave[None, :])

    dma = pltpu.SemaphoreType.DMA
    vmem = pltpu.VMEM
    whole = pl.BlockSpec(memory_space=vmem)
    recon, loglik = pl.pallas_call(
        kernel,
        out_shape=(
            jax.ShapeDtypeStruct(bank.shape, F32),
            jax.ShapeDtypeStruct((rows,), F32),
        ),
        in_specs=[pl.BlockSpec(memory_space=pl.ANY)] + [whole] * 7,
        out_specs=(whole, whole),
        scratch_shapes=[
            vmem((rows, size), BF16),
            vmem((16, 16, half), BF16),
            vmem((rows, 128), F32),
            vmem((rows, 128), F32),
            vmem((rows, 128), F32),
            vmem((rows, 128), F32),
            vmem((rows, 128), jnp.int32),
            vmem((rows, 128), F32),
            vmem((rows, 256), F32),
            vmem((16, 128), F32),
            vmem((256, size // CHUNKS), BF16),
            vmem((128, size // CHUNKS), BF16),
            vmem((128, rows), F32),
            vmem((128, rows), BF16),
            vmem((8, rows), F32),
            vmem((8, 8, rows), F32),
            vmem((16, 8, 128), F32),
            vmem((16, 8, 128), F32),
            vmem((8, 128), F32),
            vmem((2, 4, 2, 16, half), BF16),
            vmem((4, 2, 16, half), BF16),
            vmem((3, 2, 16, half // 2), BF16),
            vmem((3, 16, half // 2), BF16),
            vmem((4, 16, half // 2), BF16),
            vmem((16, half // 2), BF16),
            dma((2, CHUNKS)),
            dma,
            dma((CHUNKS,)),
            dma((3,)),
            dma((3, CHUNKS)),
            dma((4,)),
            dma((4, CHUNKS)),
            dma((8,)),
            dma((8,)),
            dma((16,)),
            dma((16,)),
            dma((2,)),
            dma((2, CHUNKS)),
            dma((8,)),
            dma((3, CHUNKS)),
            dma((3, CHUNKS)),
            dma((CHUNKS,)),
            dma((CHUNKS,)),
        ],
        compiler_params=pltpu.CompilerParams(
            collective_id=0, has_side_effects=True, vmem_limit_bytes=60 * 1024 * 1024
        ),
        name="expectation",
    )(
        images, ctf_table, noise_var.reshape(1, size), tau.reshape(1, size), bank, wave,
        shifts.T, defocus,
    )
    return recon, loglik


def solution(mesh):
    in_specs = (
        P("particle", None),
        P(),
        P("particle"),
        P("particle", None),
        P(),
        P(),
        P("classes", ("particle", "orient"), None),
    )
    out_specs = (P("classes", ("particle", "orient"), None), P("particle"))
    return jax.shard_map(body, mesh=mesh, in_specs=in_specs, out_specs=out_specs, check_vma=False)
```

```python
import jax
import jax.numpy as jnp
import numpy as np
from jax import lax
from jax.experimental import pallas as pl
from jax.experimental.pallas import tpu as pltpu
from jax.sharding import PartitionSpec as P

MESH = pl.DeviceIdType.MESH
BOX = 128
F32 = jnp.float32
BF16 = jnp.bfloat16
NT = (((1,), (1,)), ((), ()))
CHUNKS = 8
GROUP = 64
LAG = 4
STEPS = 4
STAGES = (1, 3, 5, 7)
SCORE_ROWS = 768


def pick_rows(table, index):
    parts = [
        jnp.take_along_axis(table, index[s : s + 8], axis=0, mode="promise_in_bounds")
        for s in range(0, index.shape[0], 8)
    ]
    return parts[0] if len(parts) == 1 else jnp.concatenate(parts, axis=0)


def kernel(
    images, ctf, noise, tau, bank, wave, moves, bin_row,
    recon, loglik,
    xc, gathered, cst, sst, rcos, rsin, bin_lanes, off, acc, csq, scaled, squared, scores, wt, msg, msgs, binsend, binrecv, binsum,
    part, sib, ring_a, ring_b, cross, fin,
    img_sem, ysend, yrecv, rsend, rrecv, ssend, srecv,
    msend, mrecv, bsend, brecv, psend, precv, qsend, arecv, brecv_ring, crecv, frecv,
):
    rows, size = xc.shape
    half = size // 2
    width = half // CHUNKS
    tiles = width // 128

    me = lax.axis_index("particle")
    cls = lax.axis_index("classes")
    ori = lax.axis_index("orient")
    core = me % 2
    yh = (me // 2) % 2
    x = me // 4
    turn = 3 + 2 * core
    nxt = (((x + 1 + 2 * core) % 4) * 2 + yh) * 2 + core
    prv = (((x + 3 + 2 * core) % 4) * 2 + yh) * 2 + core
    sibling = me + 1 - 2 * core
    partner = me + 2 - 4 * yh
    own = core * 8 + x * 2 + yh
    share = cls * 2 + ori

    def cols(c, base=0):
        return pl.ds(pl.multiple_of(base + c * width, width), width)

    def img_copy(h, c):
        where = cols(c, h * half)
        return pltpu.make_async_copy(images.at[:, where], xc.at[:, where], img_sem.at[h, c])

    def start_images(c, _):
        img_copy(0, c).start()
        img_copy(1, c).start()
        return 0

    lax.fori_loop(0, 2, start_images, 0)

    def share_device(s):
        return {"classes": s // 2, "orient": s % 2}

    def arrange(c, _):
        pieces = [bank[k, :, cols(c, h * half)].astype(F32) for h in range(2) for k in range(2)]
        gathered[own, :, cols(c)] = jnp.concatenate(pieces, axis=0).astype(BF16)
        return 0

    lax.fori_loop(0, CHUNKS, arrange, 0)

    barrier = pltpu.get_barrier_semaphore()
    for k in range(1, 16):
        pl.semaphore_signal(barrier, inc=1, device_id={"particle": (me + k) % 16}, device_id_type=MESH)
    for k in range(1, 8):
        pl.semaphore_signal(barrier, inc=1, device_id=share_device((share + k) % 8), device_id_type=MESH)
    pl.semaphore_wait(barrier, 22)

    def remote(src, dst, send, recv, to):
        return pltpu.make_async_remote_copy(
            src_ref=src, dst_ref=dst, send_sem=send, recv_sem=recv, device_id=to, device_id_type=MESH
        )

    def y_copy(c, q=None):
        q = cols(c) if q is None else q
        return remote(
            gathered.at[own, :, q], gathered.at[own, :, q], ysend, yrecv.at[c], {"particle": partner}
        )

    def pair(t, q):
        return gathered.at[pl.ds(core * 8 + ((x + t * turn) % 4) * 2, 2), :, q]

    def ring_copy(t, c, q=None):
        q = cols(c) if q is None else q
        block = pair(1 if t == 2 else 0, q)
        return remote(block, block, rsend.at[t], rrecv.at[t, c], {"particle": prv if t == 1 else nxt})

    def sib_copy(t, c, q=None):
        q = cols(c) if q is None else q
        return remote(pair(t, q), pair(t, q), ssend.at[t], srecv.at[t, c], {"particle": sibling})

    def start_y(c, _):
        y_copy(c).start()
        return 0

    lax.fori_loop(0, CHUNKS, start_y, 0)

    lane = lax.broadcasted_iota(jnp.int32, (128, 128), 1)

    waves = jnp.broadcast_to(wave[...], (8, BOX))

    def look(turns):
        turns = turns & (BOX - 1)
        return jnp.concatenate(
            [
                jnp.take_along_axis(waves, turns[s : s + 8], axis=1, mode="promise_in_bounds")
                for s in range(0, 128, 8)
            ],
            axis=0,
        )

    def phases(r, _):
        span = pl.ds(pl.multiple_of(r * 128, 128), 128)
        shift_x, shift_y, bins_of = [
            jnp.broadcast_to(row.astype(F32), (128, 128)).T.astype(jnp.int32)
            for row in (moves[0:1, span], moves[1:2, span], bin_row[span].reshape(1, 128))
        ]
        turns = shift_x * (lane % 64) + shift_y * (lane // 64)
        cst[span, :] = look(turns)
        sst[span, :] = look(turns - BOX // 4)
        rcos[span, :] = look(2 * shift_y)
        rsin[span, :] = look(2 * shift_y - BOX // 4)
        bin_lanes[span, :] = bins_of
        return 0

    lax.fori_loop(0, rows // 128, phases, 0)
    off[...] = jnp.zeros_like(off)
    acc[...] = jnp.zeros_like(acc)
    csq[...] = jnp.zeros_like(csq)

    def shift_chunk(c, part_of, with_offset):
        lows = [pl.multiple_of(c * width + j * 128, 128) for j in range(tiles)]

        def group(g, _):
            where = pl.ds(pl.multiple_of(g * GROUP, GROUP), GROUP)
            cosine, sine = cst[where, :], sst[where, :]
            step_c, step_s = rcos[where, :], rsin[where, :]
            index = bin_lanes[where, :]
            total = off[where, :] if with_offset else None
            for low in lows:
                at_re = pl.ds(low, 128)
                at_im = pl.ds(pl.multiple_of(half + low, 128), 128)
                re = xc[where, at_re].astype(F32)
                im = xc[where, at_im].astype(F32)
                out_re = re * cosine - im * sine
                out_im = re * sine + im * cosine
                if with_offset:
                    total = total + out_re * out_re * (0.5 / noise[:, at_re])
                    total = total + out_im * out_im * (0.5 / noise[:, at_im])
                xc[where, at_re] = (out_re * pick_rows(ctf[:, at_re], index)).astype(BF16)
                xc[where, at_im] = (out_im * pick_rows(ctf[:, at_im], index)).astype(BF16)
                cosine, sine = cosine * step_c - sine * step_s, sine * step_c + cosine * step_s
            cst[where, :] = cosine
            sst[where, :] = sine
            if with_offset:
                off[where, :] = total
            return 0

        per = rows // GROUP // 2
        lax.fori_loop(part_of * per, part_of * per + per, group, 0)

    def score(c):
        for t in range(4):
            sib_copy(t, c).wait_recv()
        for h in range(2):
            at = cols(c, h * half)
            inverse = 1.0 / noise[:, at]

            def prepare(m, _):
                b0 = gathered[2 * m, :, cols(c)].astype(F32)
                b1 = gathered[2 * m + 1, :, cols(c)].astype(F32)
                b = jnp.concatenate([b0[h * 8 : h * 8 + 8], b1[h * 8 : h * 8 + 8]], axis=0)
                value = b * inverse
                high = value.astype(BF16)
                to = pl.multiple_of(m * 16, 16)
                scaled[pl.ds(to, 16), h * width : (h + 1) * width] = high
                scaled[pl.ds(128 + to, 16), h * width : (h + 1) * width] = (value - high.astype(F32)).astype(BF16)
                squared[pl.ds(to, 16), h * width : (h + 1) * width] = (b * b).astype(BF16)
                return 0

            lax.fori_loop(0, 8, prepare, 0)
            table = ctf[:, at]
            cs = 0.5 * table * table * inverse
            cs = jnp.concatenate([cs, cs], axis=0).astype(BF16)
            csq[...] += lax.dot_general(
                cs, squared[:, h * width : (h + 1) * width], NT, preferred_element_type=F32
            )

        def block(r, _):
            where = pl.ds(pl.multiple_of(r * SCORE_ROWS, SCORE_ROWS), SCORE_ROWS)
            acc[where, :] += lax.dot_general(
                xc[where, cols(c)], scaled[:, :width], NT, preferred_element_type=F32
            ) + lax.dot_general(xc[where, cols(c, half)], scaled[:, width:], NT, preferred_element_type=F32)
            return 0

        lax.fori_loop(0, rows // SCORE_ROWS, block, 0)

    def first(n, _):
        @pl.when(n < CHUNKS)
        def _():
            y_copy(n).wait_recv()
            ring_copy(0, n).start()
            ring_copy(1, n).start()
            sib_copy(0, n).start()

        near = n - LAG

        @pl.when((near >= 0) & (near < CHUNKS))
        def _():
            ring_copy(0, near).wait_recv()
            ring_copy(2, near).start()
            sib_copy(1, near).start()
            ring_copy(1, near).wait_recv()
            sib_copy(3, near).start()

        far = n - 2 * LAG

        @pl.when((far >= 0) & (far < CHUNKS))
        def _():
            ring_copy(2, far).wait_recv()
            sib_copy(2, far).start()

        c = n // 2
        part_of = n % 2
        shifting = n < 2 * CHUNKS

        @pl.when(shifting & (part_of == 0))
        def _():
            @pl.when(c + 2 < CHUNKS)
            def _():
                start_images(c + 2, 0)

            img_copy(0, c).wait()
            img_copy(1, c).wait()

        @pl.when(shifting & (c == share))
        def _():
            shift_chunk(c, part_of, True)

        @pl.when(shifting & (c != share))
        def _():
            shift_chunk(c, part_of, False)

        ready = n - 2 * LAG - 2

        @pl.when((ready >= 0) & (ready < CHUNKS))
        def _():
            score(ready)

        return 0

    lax.fori_loop(0, max(2 * LAG + 2 + CHUNKS, 2 * CHUNKS), first, 0)

    penalty = csq[0:8, :]
    lanes = rows // 128
    msg[...] = jnp.zeros_like(msg)
    for r in range(lanes):
        span = slice(r * 128, (r + 1) * 128)
        block_scores = acc[span, 0:128] + acc[span, 128:256] - pick_rows(penalty, bin_lanes[span, :])
        block_scores = block_scores.T
        scores[:, span] = block_scores
        block_top = jnp.max(block_scores, axis=0, keepdims=True)
        msg[r : r + 1, :] = block_top
        msg[8 + r : 9 + r, :] = jnp.sum(jnp.exp(block_scores - block_top), axis=0, keepdims=True)
        msg[16 + r : 17 + r, :] = jnp.sum(off[span, :].T, axis=0, keepdims=True)

    def share_copy(k):
        return remote(msg, msgs.at[k], msend.at[k], mrecv.at[k], share_device((share + k) % 8))

    for k in range(1, 8):
        share_copy(k).start()
    msgs[0] = msg[...]
    for k in range(1, 8):
        share_copy(k).wait_recv()
    top = msgs[0, 0:8, :]
    for k in range(1, 8):
        top = jnp.maximum(top, msgs[k, 0:8, :])
    total = jnp.zeros_like(top)
    offset = jnp.zeros_like(top)
    for k in range(8):
        total = total + msgs[k, 8:16, :] * jnp.exp(msgs[k, 0:8, :] - top)
        offset = offset + msgs[k, 16:24, :]
    found = top + jnp.log(total) - offset
    for r in range(lanes):
        span = slice(r * 128, (r + 1) * 128)
        loglik[span] = found[r : r + 1, :].reshape(128)
        wt[:, span] = (jnp.exp(scores[:, span] - top[r : r + 1, :]) / total[r : r + 1, :]).astype(BF16)
    onehot = jnp.where(lax.broadcasted_iota(jnp.int32, (128, rows), 0) == bin_row[...].reshape(1, rows), 1.0, 0.0).astype(BF16)
    bins = lax.dot_general(wt[...], onehot, NT, preferred_element_type=F32)
    for u in range(16):
        binsend[u] = bins[u * 8 : u * 8 + 8, :]

    def bin_copy(k):
        to = (me + k) % 16
        slot = (to % 2) * 8 + (to // 4) * 2 + (to // 2) % 2
        return remote(binsend.at[slot], binrecv.at[k], bsend.at[k], brecv.at[k], {"particle": to})

    for k in range(1, 16):
        bin_copy(k).start()

    steps = STEPS
    middle = half // 2
    span_of = middle // steps
    sub = min(512, span_of)

    def at_step(route, d):
        return pl.ds(pl.multiple_of(route * middle + d * span_of, span_of), span_of)

    def local(d):
        return pl.ds(pl.multiple_of(d * span_of, span_of), span_of)

    def everything(route):
        return pl.ds(route * middle, middle)

    def part_copy(route, d, q=None):
        q = at_step(route, d) if q is None else q
        return remote(
            part.at[1 - core, :, :, :, q], sib.at[:, :, :, q],
            psend.at[route], precv.at[route, d], {"particle": sibling},
        )

    onward, across, behind = (x + 3 * turn) % 4, (x + 2) % 4, (x + turn) % 4
    goal = (across, behind, onward)
    to = (nxt, prv, nxt)

    def ring_a_copy(t, d, q=None):
        p = local(d) if q is None else q
        q = at_step(0, d) if q is None else q
        return remote(
            part.at[core, goal[t], :, :, q], ring_a.at[t, :, :, p],
            qsend.at[t], arecv.at[t, d], {"particle": to[t]},
        )

    def fin_copy(d, q=None):
        p = local(d) if q is None else q
        q = at_step(0, d) if q is None else q
        return remote(
            part.at[core, x, 1 - yh, :, q], fin.at[:, p], qsend.at[3], frecv.at[d], {"particle": partner}
        )

    def cross_copy(d, whole=False):
        p = everything(0) if whole else local(d)
        q = everything(1) if whole else at_step(1, d)
        return remote(
            part.at[core, :, 1 - yh, :, q], cross.at[:, :, p], qsend.at[4], crecv.at[d], {"particle": partner}
        )

    def ring_b_copy(t, d, whole=False):
        p = everything(0) if whole else local(d)
        q = everything(1) if whole else at_step(1, d)
        return remote(
            part.at[core, goal[t], yh, :, q], ring_b.at[t, :, p],
            qsend.at[5 + t], brecv_ring.at[t, d], {"particle": to[t]},
        )

    def gain(i, j, q, *others):
        value = part[core, i, j, :, q].astype(F32)
        for other in others:
            value = value + other.astype(F32)
        part[core, i, j, :, q] = value.astype(BF16)

    def result(route, d, *others):
        q = at_step(route, d)
        both = part[core, x, yh, :, q].astype(F32)
        for other in others:
            both = both + other.astype(F32)
        for h in range(2):
            at = pl.ds(pl.multiple_of(h * half + route * middle + d * span_of, span_of), span_of)
            below = jnp.broadcast_to(tau[:, at], (8, span_of))
            for b in range(8):
                value = ctf[b : b + 1, at]
                below = below + binsum[:, b : b + 1] * (value * value)
            value = both[h * 8 : h * 8 + 8] / below
            recon[0, :, at] = value[0:4]
            recon[1, :, at] = value[4:8]

    def stage(n, lag):
        d = n - lag
        return d, pl.when((d >= 0) & (d < steps))

    def second(n, _):
        @pl.when(n < steps)
        def _():
            per = span_of // sub

            def piece(s, _):
                low = (s // per) * middle + n * span_of + (s % per) * sub
                at = pl.ds(pl.multiple_of(low, sub), sub)
                at_im = pl.ds(pl.multiple_of(half + low, sub), sub)
                re = jnp.dot(wt[...], xc[:, at], preferred_element_type=F32)
                im = jnp.dot(wt[...], xc[:, at_im], preferred_element_type=F32)
                for u in range(16):
                    span = slice(u * 8, u * 8 + 8)
                    part[u // 8, (u // 2) % 4, u % 2, :, at] = jnp.concatenate(
                        [re[span], im[span]], axis=0
                    ).astype(BF16)
                return 0

            lax.fori_loop(0, 2 * per, piece, 0)
            part_copy(0, n).start()
            part_copy(1, n).start()

        d1, on1 = stage(n, STAGES[0])

        @on1
        def _():
            for route in range(2):
                part_copy(route, d1).wait_recv()
                q = at_step(route, d1)

                def add(i, _):
                    for j in range(2):
                        gain(i, j, q, sib[i, j, :, q])
                    return 0

                lax.fori_loop(0, 4, add, 0)
                if route == 0:
                    ring_a_copy(0, d1).start()
                    ring_a_copy(1, d1).start()
                else:
                    cross_copy(d1).start()

        d2, on2 = stage(n, STAGES[1])

        @on2
        def _():
            ring_a_copy(0, d2).wait_recv()
            for j in range(2):
                gain(onward, j, at_step(0, d2), ring_a[0, j, :, local(d2)])
            ring_a_copy(2, d2).start()
            cross_copy(d2).wait_recv()
            for i in range(4):
                gain(i, yh, at_step(1, d2), cross[i, :, local(d2)])
            ring_b_copy(0, d2).start()
            ring_b_copy(1, d2).start()

        d3, on3 = stage(n, STAGES[2])

        @on3
        def _():
            ring_b_copy(0, d3).wait_recv()
            gain(onward, yh, at_step(1, d3), ring_b[0, :, local(d3)])
            ring_b_copy(2, d3).start()
            ring_a_copy(1, d3).wait_recv()
            ring_a_copy(2, d3).wait_recv()
            for j in range(2):
                gain(x, j, at_step(0, d3), ring_a[1, j, :, local(d3)], ring_a[2, j, :, local(d3)])
            fin_copy(d3).start()

        @pl.when(n == STAGES[3] - 1)
        def _():
            whole = binsend[own]
            for k in range(1, 16):
                bin_copy(k).wait_recv()
                whole = whole + binrecv[k]
            binsum[...] = whole

        d4, on4 = stage(n, STAGES[3])

        @on4
        def _():
            fin_copy(d4).wait_recv()
            result(0, d4, fin[:, local(d4)])
            ring_b_copy(1, d4).wait_recv()
            ring_b_copy(2, d4).wait_recv()
            result(1, d4, ring_b[1, :, local(d4)], ring_b[2, :, local(d4)])

        return 0

    lax.fori_loop(0, steps + STAGES[3], second, 0)

    full = pl.ds(0, half)
    y_copy(0, full).wait_send()
    for t in range(3):
        ring_copy(t, 0, full).wait_send()
        ring_a_copy(t, 0, everything(0)).wait_send()
        ring_b_copy(t, 0, True).wait_send()
    for t in range(4):
        sib_copy(t, 0, full).wait_send()
    for route in range(2):
        part_copy(route, 0, everything(route)).wait_send()
    fin_copy(0, everything(0)).wait_send()
    cross_copy(0, True).wait_send()
    for k in range(1, 8):
        share_copy(k).wait_send()
    for k in range(1, 16):
        bin_copy(k).wait_send()


def hand_over(recon, loglik, recon_out, loglik_out):
    recon_out[...] = recon[...]
    loglik_out[...] = loglik[...]


def body(images, ctf_table, defocus, shifts, noise_var, tau, bank):
    rows, size = images.shape
    half = size // 2
    wave = np.cos(2.0 * np.pi / BOX * np.arange(BOX)).astype(np.float32)
    wave = jnp.asarray(wave[None, :])

    dma = pltpu.SemaphoreType.DMA
    vmem = pltpu.VMEM
    whole = pl.BlockSpec(memory_space=vmem)
    recon, loglik = pl.pallas_call(
        kernel,
        out_shape=(
            jax.ShapeDtypeStruct(bank.shape, F32),
            jax.ShapeDtypeStruct((rows,), F32),
        ),
        in_specs=[pl.BlockSpec(memory_space=pl.ANY)] + [whole] * 7,
        out_specs=(whole, whole),
        scratch_shapes=[
            vmem((rows, size), BF16),
            vmem((16, 16, half), BF16),
            vmem((rows, 128), F32),
            vmem((rows, 128), F32),
            vmem((rows, 128), F32),
            vmem((rows, 128), F32),
            vmem((rows, 128), jnp.int32),
            vmem((rows, 128), F32),
            vmem((rows, 256), F32),
            vmem((16, 128), F32),
            vmem((256, size // CHUNKS), BF16),
            vmem((128, size // CHUNKS), BF16),
            vmem((128, rows), F32),
            vmem((128, rows), BF16),
            vmem((24, 128), F32),
            vmem((8, 24, 128), F32),
            vmem((16, 8, 128), F32),
            vmem((16, 8, 128), F32),
            vmem((8, 128), F32),
            vmem((2, 4, 2, 16, half), BF16),
            vmem((4, 2, 16, half), BF16),
            vmem((3, 2, 16, half // 2), BF16),
            vmem((3, 16, half // 2), BF16),
            vmem((4, 16, half // 2), BF16),
            vmem((16, half // 2), BF16),
            dma((2, CHUNKS)),
            dma,
            dma((CHUNKS,)),
            dma((3,)),
            dma((3, CHUNKS)),
            dma((4,)),
            dma((4, CHUNKS)),
            dma((8,)),
            dma((8,)),
            dma((16,)),
            dma((16,)),
            dma((2,)),
            dma((2, STEPS)),
            dma((8,)),
            dma((3, STEPS)),
            dma((3, STEPS)),
            dma((STEPS,)),
            dma((STEPS,)),
        ],
        compiler_params=pltpu.CompilerParams(
            collective_id=0, has_side_effects=True, vmem_limit_bytes=60 * 1024 * 1024
        ),
        name="expectation",
    )(
        images, ctf_table, noise_var.reshape(1, size), tau.reshape(1, size), bank, wave,
        shifts.T, defocus,
    )
    recon, loglik = pl.pallas_call(
        hand_over,
        out_shape=(jax.ShapeDtypeStruct(bank.shape, F32), jax.ShapeDtypeStruct((rows,), F32)),
        in_specs=[whole, whole],
        out_specs=(whole, whole),
        name="hand_over",
    )(recon, loglik)
    return recon, loglik


def solution(mesh):
    in_specs = (
        P("particle", None),
        P(),
        P("particle"),
        P("particle", None),
        P(),
        P(),
        P("classes", ("particle", "orient"), None),
    )
    out_specs = (P("classes", ("particle", "orient"), None), P("particle"))
    return jax.shard_map(body, mesh=mesh, in_specs=in_specs, out_specs=out_specs, check_vma=False)
```
